128 devices in a mesh: row: 8 (over z, core), col: 16 (over y, x).
Axes of the slice: x: 4, y: 4, z: 4, core: 2. Of those that a mesh axis runs over, the one named last changes fastest.
Arguments:
- start: float32 [98304, 32], P(('row', 'col')), may hold values from -410 to 410
- self_weight: float32 [98304], P(('row', 'col')), may hold values from 1 to 3
- blocks: bfloat16 [8, 16, 128, 256, 256], P('row', 'col'), may hold values from -0.0625 to 0.0625
- slot_row: int32 [8, 16, 128], P('row', 'col'), may hold values from 0 to 47, as said below
- slot_col: int32 [8, 16, 128], P('row', 'col'), may hold values from 0 to 23
- slot_count: int32 [8, 16], P('row', 'col'), may hold values from 3 to 128, as said below
Outputs:
- basis: float32 [98304, 32], P(('row', 'col'))
The draws below stay inside these ranges and needn't reach their ends.
Inputs may be any that keep to these rules, and one draw needn't show every extreme that they name: `slot_row`: slots that a grid position uses name distinct blocks with I < J. `slot_count`: some position of grid row 0 uses all 128 slots.
All inputs are finite; a program needn't handle non-finite values.
Results may differ from the reference program's by a relative error of at most 0.0021.
Values may be sent and summed in bfloat16 or wider, within the bound.
A program may use at most 128 MiB of HBM per device.

```python
import math
import jax
import jax.numpy as jnp
from jax import lax

B = 256
K = 32
ITERS = 2
BLK_DEV = 3
CAP = 128
NB = 384
NROWS = 98304
ROWG = 48
COLG = 24
N_ROW = 8
N_COL = 16


def slot_pairs(key):
    pairs = ROWG * COLG
    index = jnp.arange(pairs, dtype=jnp.int32)
    row_pos = index // COLG
    col_pos = index % COLG
    grid_rows = jnp.arange(N_ROW, dtype=jnp.int32)[:, None, None]
    grid_cols = jnp.arange(N_COL, dtype=jnp.int32)[None, :, None]
    block_row = grid_rows * ROWG + row_pos[None, None, :]
    block_col = (col_pos // BLK_DEV)[None, None, :] * ROWG + grid_cols * BLK_DEV + (col_pos % BLK_DEV)[None, None, :]
    eligible = block_row < block_col
    scores = jax.random.randint(jax.random.fold_in(key, 17), (N_ROW, N_COL, pairs), 0, 2 ** 30 // pairs) * pairs + index
    ranked = jnp.where(eligible, scores, scores - 2 ** 30)
    picked = lax.top_k(ranked, CAP)[1].astype(jnp.int32)
    return (picked // COLG, picked % COLG, jnp.sum(eligible.astype(jnp.int32), axis=2))


def draw_slot_row(key, part):
    picked_rows, picked_cols, eligible = slot_pairs(key)
    return picked_rows


def draw_slot_col(key, part):
    picked_rows, picked_cols, eligible = slot_pairs(key)
    return picked_cols


def draw_slot_count(key, part):
    picked_rows, picked_cols, eligible = slot_pairs(key)
    key = jax.random.fold_in(key, 2)
    wanted = jax.random.randint(key, (N_ROW, N_COL), CAP // 2, CAP + 1)
    chosen = jax.random.randint(jax.random.fold_in(key, 3), (), 0, N_COL)
    wanted = wanted.at[0, chosen].set(CAP)
    return jnp.minimum(wanted, eligible).astype(jnp.int32)


def draw_start(key, part):
    key = jax.random.fold_in(key, 5)
    subkeys = jax.random.split(key, 3)
    row_scale = jnp.exp(jax.random.uniform(subkeys[1], (NROWS, 1)) * math.log(10.0))
    col_scale = jnp.exp(jax.random.uniform(subkeys[2], (1, K)) * math.log(10.0))
    values = jax.random.truncated_normal(subkeys[0], -4.0, 4.0, (NROWS, K))
    return (values * row_scale * col_scale).astype(jnp.float32)


def block_scale(key, dims, cuts, smallest, high):
    def one(axis_at, parts):
        heights = jax.random.uniform(jax.random.fold_in(jax.random.fold_in(key, 6), axis_at), (parts,), jnp.float32, smallest / len(cuts), high / len(cuts))
        return jnp.repeat(jnp.exp(heights), dims[axis_at] // parts).reshape((-1,) + (1,) * (len(dims) - axis_at - 1))

    level = one(*cuts[0])
    for cut in cuts[1:]:
        level = level * one(*cut)
    return level


def bell_draw(key, shape, scale, most, cuts=(), held_as=jnp.bfloat16):
    array = jax.random.normal(key, shape, jnp.float32) * scale
    if len(cuts) > 0:
        array = block_scale(key, shape, cuts, -0.22, 0.18) * array
    return jnp.clip(array, min=-most, max=most).astype(held_as)


def setup_inputs(seed: int = 0) -> dict:
    splits = jax.random.split(jax.random.key(seed), 7)
    start = draw_start(jax.random.fold_in(splits[6], 71), 0)
    self_weight = jnp.clip(1.0 + 2.0 * jax.random.uniform(splits[1], (NROWS,), jnp.float32) ** block_scale(splits[1], (NROWS,), ((0, 128),), -0.2, 0.2), 1.0, 3.0)
    blocks = bell_draw(splits[2], (N_ROW, N_COL, CAP, B, B), (B * CAP // 4) ** -0.5, 0.0625, ((0, 8), (1, 16)))
    slot_row = draw_slot_row(jax.random.fold_in(splits[6], 71), 0)
    slot_col = draw_slot_col(jax.random.fold_in(splits[6], 71), 0)
    slot_count = draw_slot_count(jax.random.fold_in(splits[6], 71), 0)
    return dict(start=start, self_weight=self_weight, blocks=blocks, slot_row=slot_row, slot_col=slot_col, slot_count=slot_count)


def slot_products(stored, rows_here, cols_here, used, grid_row, grid_col, rounded):
    live_slots = (jnp.arange(CAP) < used).astype(jnp.float32)
    block_row = (grid_row * ROWG + rows_here).astype(jnp.int32)
    block_col = (cols_here // BLK_DEV * ROWG + grid_col * BLK_DEV + cols_here % BLK_DEV).astype(jnp.int32)
    wide_blocks = stored.astype(jnp.float32)
    far_vectors = rounded[block_col].astype(jnp.float32)
    near_vectors = rounded[block_row].astype(jnp.float32)
    forward = jnp.einsum('sab,sbk->sak', wide_blocks, far_vectors) * live_slots[:, None, None]
    backward = jnp.einsum('sab,sak->sbk', wide_blocks, near_vectors) * live_slots[:, None, None]
    return (block_row, block_col, forward, backward)

def reference(start, self_weight, blocks, slot_row, slot_col, slot_count):
    positions = N_ROW * N_COL
    flat_blocks = blocks.reshape(positions, CAP, B, B)
    flat_rows = slot_row.reshape(positions, CAP)
    flat_cols = slot_col.reshape(positions, CAP)
    flat_counts = slot_count.reshape(positions)
    grid_rows = (jnp.arange(positions) // N_COL).astype(jnp.int32)
    grid_cols = (jnp.arange(positions) % N_COL).astype(jnp.int32)
    basis = start
    for iteration in range(ITERS):
        rounded = basis.astype(jnp.bfloat16).reshape(NB, B, K)

        def accumulate(totals, item):
            stored, rows_here, cols_here, used, grid_row, grid_col = item
            block_row, block_col, forward, backward = slot_products(stored, rows_here, cols_here, used, grid_row, grid_col, rounded)
            totals = totals.at[block_row].add(forward).at[block_col].add(backward)
            return (totals, None)
        totals, unused = lax.scan(accumulate, jnp.zeros((NB, B, K), jnp.float32), (flat_blocks, flat_rows, flat_cols, flat_counts, grid_rows, grid_cols))
        image = self_weight[:, None] * basis + totals.reshape(NROWS, K)
        gram_matrix = jnp.dot(image.T.astype(jnp.float32), image.astype(jnp.float32), precision=lax.Precision.HIGHEST, preferred_element_type=jnp.float32) / NROWS
        factor = jnp.linalg.cholesky(gram_matrix)
        basis = jax.scipy.linalg.solve_triangular(factor, image.T, lower=True).T
    return basis
```

```python
import functools

import jax
import jax.numpy as jnp
from jax import lax
from jax.experimental import pallas as pl
from jax.experimental.pallas import tpu as pltpu
from jax.sharding import PartitionSpec as P

ITERS = 2
MESH = pl.DeviceIdType.MESH
NT = (((1,), (1,)), ((), ()))
NN = (((1,), (0,)), ((), ()))
HIGH = lax.Precision.HIGHEST
F32 = jnp.float32
BF16 = jnp.bfloat16
UNROLL = 32
CHUNKS = 16


def sort_slots(keys, partner, spare):
    n = keys.shape[1]
    lane = lax.broadcasted_iota(jnp.int32, (n, n), 1)
    slot = lax.broadcasted_iota(jnp.int32, (n, n), 0)

    def down(row):
        return jnp.broadcast_to(row, (n, n)).T

    def total(mask, value):
        return jnp.sum(jnp.where(mask, value, 0), axis=0, keepdims=True)

    key_down = down(keys)
    key_across = jnp.broadcast_to(keys, (n, n))
    ahead = (key_down < key_across) | ((key_down == key_across) & (slot < lane))
    rank = total(ahead, 1)
    placed = down(rank) == lane
    order = total(placed, slot)
    other = total(placed, down(partner))
    ordered = total(placed, key_down)
    first_lane = lax.broadcasted_iota(jnp.int32, (1, n), 1)
    before = pltpu.roll(ordered, 1, 1)
    keep = jnp.where((first_lane > 0) & (before == ordered), 1, 0)
    last = total(key_down <= lane, 1) - 1
    last = jnp.where(total(key_down == lane, 1) > 0, last, spare)
    return order, other, keep, last


def inverse_factor(gram):
    k = gram.shape[0]
    row = lax.broadcasted_iota(jnp.int32, (k, 2 * k), 0)
    eye = (lax.broadcasted_iota(jnp.int32, (k, k), 0) == lax.broadcasted_iota(jnp.int32, (k, k), 1)).astype(F32)
    work = jnp.concatenate([gram, eye], axis=1)
    for j in range(k):
        scale = lax.rsqrt(work[j : j + 1, j : j + 1])
        pivot = work[j : j + 1, :] * scale
        column = work[:, j : j + 1] * scale
        work = jnp.where(row > j, work - column * pivot, jnp.where(row == j, pivot, work))
    return work[:, k:]


def kernel(
    grid_rows, grid_cols, total_rows,
    start_ref, weight_ref, blocks_ref, slot_row_ref, slot_col_ref, count_ref, out_ref,
    start_v, held, turned, index_v, index_s, row_vecs, col_vecs, sums, row_out, col_out,
    row_in, col_in, gram_row, gram_col,
    start_sem, block_sem, index_sem,
    row_vec_send, row_vec_recv, col_vec_send, col_vec_recv,
    row_out_send, row_out_recv, col_out_send, col_out_recv,
    gram_row_send, gram_row_recv, gram_col_send, gram_col_recv,
):
    r = lax.axis_index("row")
    c = lax.axis_index("col")
    slots, side, _ = held.shape
    owned = row_in.shape[2]
    k = start_v.shape[0]
    group_rows = owned * grid_cols
    group_cols = owned * grid_rows
    per_chunk = slots // CHUNKS

    def row_peer(n):
        return lax.rem(r + n, grid_rows)

    def col_peer(n):
        return lax.rem(c + n, grid_cols)

    start_copy = pltpu.make_async_copy(start_ref, start_v, start_sem)
    start_copy.start()
    block_copies = []
    for n in range(CHUNKS):
        part = pl.ds(n * per_chunk, per_chunk)
        block_copies.append(pltpu.make_async_copy(blocks_ref.at[part], held.at[part], block_sem.at[n]))
        block_copies[-1].start()

    barrier = pltpu.get_barrier_semaphore()
    for n in range(1, grid_rows):
        pl.semaphore_signal(barrier, inc=1, device_id=(row_peer(n), c), device_id_type=MESH)
    for n in range(1, grid_cols):
        pl.semaphore_signal(barrier, inc=1, device_id=(r, col_peer(n)), device_id_type=MESH)

    lane = lax.broadcasted_iota(jnp.int32, (1, slots), 1)
    live = lane < count_ref[0, 0]
    slot_row = slot_row_ref[0]
    slot_col = slot_col_ref[0]
    for base, (keys, partner) in enumerate(
        ((jnp.where(live, slot_row, group_rows), slot_col), (jnp.where(live, slot_col, group_cols), slot_row))
    ):
        for n, found in enumerate(sort_slots(keys, partner, slots)):
            index_v[base * 4 + n : base * 4 + n + 1, :] = found
    index_copy = pltpu.make_async_copy(index_v, index_s, index_sem)
    index_copy.start()

    zeros = jnp.zeros((k, side), F32)
    sums[0, slots] = zeros
    sums[1, slots] = zeros

    start_copy.wait()
    basis = start_v[...]

    def share(it, basis):
        copies = []
        for b in range(owned):
            rounded = basis[:, b * side : (b + 1) * side].astype(BF16)
            row_vecs[it, c, b] = rounded
            col_vecs[it, r, b] = rounded
        if it == 0:
            pl.semaphore_wait(barrier, grid_rows + grid_cols - 2)
        for n in range(1, grid_rows):
            copies.append(
                pltpu.make_async_remote_copy(
                    col_vecs.at[it, r], col_vecs.at[it, r], col_vec_send.at[it, n], col_vec_recv.at[it, n],
                    device_id=(row_peer(n), c), device_id_type=MESH,
                )
            )
        for n in range(1, grid_cols):
            copies.append(
                pltpu.make_async_remote_copy(
                    row_vecs.at[it, c], row_vecs.at[it, c], row_vec_send.at[it, n], row_vec_recv.at[it, n],
                    device_id=(r, col_peer(n)), device_id_type=MESH,
                )
            )
        for copy in copies:
            copy.start()
        return copies[: grid_rows - 1], copies[grid_rows - 1 :]

    def multiply(which, matrices, vectors, it, parts):
        def some(g, running):
            for u in range(UNROLL):
                s = g * UNROLL + u
                matrix = matrices[index_s[which * 4, s]]
                q = index_s[which * 4 + 1, s]
                vector = vectors[it, q // owned, q % owned]
                product = lax.dot_general(vector, matrix, NN, preferred_element_type=F32)
                running = running * index_s[which * 4 + 2, s].astype(F32) + product
                sums[which, s] = running
            return running

        lax.fori_loop(0, slots // UNROLL, some, zeros)

    def spread(it, which, size, here, staged, landed, send, recv, place):
        copies = []
        for n in range(1, size):
            to = lax.rem(here + n, size)
            for b in range(owned):
                staged[it, to, b] = sums[which, index_s[which * 4 + 3, to * owned + b]].astype(BF16)
            copies.append(
                pltpu.make_async_remote_copy(
                    staged.at[it, to], landed.at[it, here], send.at[it, n], recv.at[it, n],
                    device_id=place(to), device_id_type=MESH,
                )
            )
            copies[-1].start()
        return copies

    def reduce_gram(it, part, landed, size, here, send, recv, place):
        landed[it, here] = part
        copies = []
        for n in range(1, size):
            to = lax.rem(here + n, size)
            copies.append(
                pltpu.make_async_remote_copy(
                    landed.at[it, here], landed.at[it, here], send.at[it, n], recv.at[it, n],
                    device_id=place(to), device_id_type=MESH,
                )
            )
            copies[-1].start()
        for copy in copies:
            copy.wait()
        total = landed[it, 0]
        for n in range(1, size):
            total = total + landed[it, n]
        return total

    for it in range(ITERS):
        col_copies, row_copies = share(it, basis)
        if it == 0:
            index_copy.wait()
            for n in range(CHUNKS):
                block_copies[n].wait()

                def turn(m, _, n=n):
                    turned[n * per_chunk + m] = held[n * per_chunk + m].T
                    return 0

                lax.fori_loop(0, per_chunk, turn, 0, unroll=True)
        for copy in col_copies:
            copy.wait()
        multiply(0, turned, col_vecs, it, None)
        row_moves = spread(
            it, 0, grid_cols, c, row_out, row_in, row_out_send, row_out_recv, lambda to: (r, to)
        )
        for copy in row_copies:
            copy.wait()
        multiply(1, held, row_vecs, it, None)
        col_moves = spread(
            it, 1, grid_rows, r, col_out, col_in, col_out_send, col_out_recv, lambda to: (to, c)
        )
        image = []
        for b in range(owned):
            part = basis[:, b * side : (b + 1) * side]
            weight = weight_ref[pl.ds(b * side, side)].reshape(1, side)
            image.append(
                part * weight + sums[0, index_s[3, c * owned + b]] + sums[1, index_s[7, r * owned + b]]
            )
        for copy in row_moves:
            copy.wait()
        for n in range(1, grid_cols):
            at = col_peer(n)
            for b in range(owned):
                image[b] = image[b] + row_in[it, at, b].astype(F32)
        for copy in col_moves:
            copy.wait()
        for n in range(1, grid_rows):
            at = row_peer(n)
            for b in range(owned):
                image[b] = image[b] + col_in[it, at, b].astype(F32)
        image = jnp.concatenate(image, axis=1)
        gram = lax.dot_general(image, image, NT, precision=HIGH, preferred_element_type=F32)
        packed = jnp.concatenate([gram[n * 8 : n * 8 + 8] for n in range(k // 8)], axis=1)
        packed = reduce_gram(
            it, packed, gram_row, grid_rows, r, gram_row_send, gram_row_recv, lambda to: (to, c)
        )
        packed = reduce_gram(
            it, packed, gram_col, grid_cols, c, gram_col_send, gram_col_recv, lambda to: (r, to)
        )
        gram = jnp.concatenate([packed[:, n * k : n * k + k] for n in range(k // 8)], axis=0)
        inverse = inverse_factor(gram * (1.0 / total_rows))
        basis = lax.dot_general(inverse, image, NN, precision=HIGH, preferred_element_type=F32)
    out_ref[...] = basis


def solution(mesh):
    grid_rows, grid_cols = mesh.shape["row"], mesh.shape["col"]

    def shards(start, self_weight, blocks, slot_row, slot_col, slot_count):
        rows, k = start.shape
        slots, side = blocks.shape[2], blocks.shape[3]
        owned = rows // side
        group_rows, group_cols = owned * grid_cols, owned * grid_rows
        total_rows = rows * grid_rows * grid_cols
        any_space = pl.BlockSpec(memory_space=pl.ANY)
        vmem = pl.BlockSpec(memory_space=pltpu.VMEM)
        dma = pltpu.SemaphoreType.DMA
        turned = pl.pallas_call(
            functools.partial(kernel, grid_rows, grid_cols, total_rows),
            out_shape=jax.ShapeDtypeStruct((k, rows), F32),
            in_specs=[any_space, vmem, any_space, vmem, vmem, pl.BlockSpec(memory_space=pltpu.SMEM)],
            out_specs=vmem,
            scratch_shapes=[
                pltpu.VMEM((k, rows), F32),
                pltpu.VMEM((slots, side, side), BF16),
                pltpu.VMEM((slots, side, side), BF16),
                pltpu.VMEM((8, slots), jnp.int32),
                pltpu.SMEM((8, slots), jnp.int32),
                pltpu.VMEM((ITERS, grid_cols, owned, k, side), BF16),
                pltpu.VMEM((ITERS, grid_rows, owned, k, side), BF16),
                pltpu.VMEM((2, slots + 1, k, side), F32),
                pltpu.VMEM((ITERS, grid_cols, owned, k, side), BF16),
                pltpu.VMEM((ITERS, grid_rows, owned, k, side), BF16),
                pltpu.VMEM((ITERS, grid_cols, owned, k, side), BF16),
                pltpu.VMEM((ITERS, grid_rows, owned, k, side), BF16),
                pltpu.VMEM((ITERS, grid_rows, 8, k * k // 8), F32),
                pltpu.VMEM((ITERS, grid_cols, 8, k * k // 8), F32),
                dma,
                dma((CHUNKS,)),
                dma,
            ]
            + [dma((ITERS, n)) for n in (grid_cols, grid_cols, grid_rows, grid_rows)] * 2
            + [dma((ITERS, n)) for n in (grid_rows, grid_rows, grid_cols, grid_cols)],
            compiler_params=pltpu.CompilerParams(
                collective_id=0, has_side_effects=True, vmem_limit_bytes=60 * 2**20
            ),
        )(
            start.T,
            self_weight,
            blocks.reshape(slots, side, side),
            slot_row.reshape(1, 1, slots),
            slot_col.reshape(1, 1, slots),
            slot_count,
        )
        return turned.T

    placed = (
        P(("row", "col"), None),
        P(("row", "col")),
        P("row", "col", None, None, None),
        P("row", "col", None),
        P("row", "col", None),
        P("row", "col"),
    )
    return jax.shard_map(
        shards, mesh=mesh, in_specs=placed, out_specs=P(("row", "col"), None), check_vma=False
    )
```

```python
import functools

import jax
import jax.numpy as jnp
from jax import lax
from jax.experimental import pallas as pl
from jax.experimental.pallas import tpu as pltpu
from jax.sharding import PartitionSpec as P

ITERS = 2
MESH = pl.DeviceIdType.MESH
NT = (((1,), (1,)), ((), ()))
NN = (((1,), (0,)), ((), ()))
HIGH = lax.Precision.HIGHEST
F32 = jnp.float32
BF16 = jnp.bfloat16
UNROLL = 32
CHUNKS = 16


def sort_slots(keys, partner, spare):
    n = keys.shape[1]
    lane = lax.broadcasted_iota(jnp.int32, (n, n), 1)
    slot = lax.broadcasted_iota(jnp.int32, (n, n), 0)

    def down(row):
        return jnp.broadcast_to(row, (n, n)).T

    def total(mask, value):
        return jnp.sum(jnp.where(mask, value, 0), axis=0, keepdims=True)

    key_down = down(keys)
    key_across = jnp.broadcast_to(keys, (n, n))
    ahead = (key_down < key_across) | ((key_down == key_across) & (slot < lane))
    rank = total(ahead, 1)
    placed = down(rank) == lane
    order = total(placed, slot)
    other = total(placed, down(partner))
    ordered = total(placed, key_down)
    first_lane = lax.broadcasted_iota(jnp.int32, (1, n), 1)
    before = pltpu.roll(ordered, 1, 1)
    keep = jnp.where((first_lane > 0) & (before == ordered), 1, 0)
    last = total(key_down <= lane, 1) - 1
    last = jnp.where(total(key_down == lane, 1) > 0, last, spare)
    return order, other, keep, last


def inverse_factor(gram):
    k = gram.shape[0]
    row = lax.broadcasted_iota(jnp.int32, (k, 2 * k), 0)
    eye = (lax.broadcasted_iota(jnp.int32, (k, k), 0) == lax.broadcasted_iota(jnp.int32, (k, k), 1)).astype(F32)
    work = jnp.concatenate([gram, eye], axis=1)
    for j in range(k):
        scale = lax.rsqrt(work[j : j + 1, j : j + 1])
        pivot = work[j : j + 1, :] * scale
        column = work[:, j : j + 1] * scale
        work = jnp.where(row > j, work - column * pivot, jnp.where(row == j, pivot, work))
    return work[:, k:]


def kernel(
    grid_rows, grid_cols, total_rows,
    start_ref, weight_ref, blocks_ref, slot_row_ref, slot_col_ref, count_ref, out_ref,
    start_v, held, turned, index_v, index_s, row_vecs, col_vecs, sums, row_out, col_out,
    row_in, col_in, gram_row, gram_col,
    start_sem, block_sem, index_sem,
    row_vec_send, row_vec_recv, col_vec_send, col_vec_recv,
    row_out_send, row_out_recv, col_out_send, col_out_recv,
    gram_row_send, gram_row_recv, gram_col_send, gram_col_recv,
):
    r = lax.axis_index("row")
    c = lax.axis_index("col")
    slots, side, _ = held.shape
    owned = row_in.shape[2]
    k = start_v.shape[0]
    group_rows = owned * grid_cols
    group_cols = owned * grid_rows
    per_chunk = slots // CHUNKS

    def row_peer(n):
        return lax.rem(r + n, grid_rows)

    def col_peer(n):
        return lax.rem(c + n, grid_cols)

    start_copy = pltpu.make_async_copy(start_ref, start_v, start_sem)
    start_copy.start()
    block_copies = []
    for n in range(CHUNKS):
        part = pl.ds(n * per_chunk, per_chunk)
        block_copies.append(pltpu.make_async_copy(blocks_ref.at[part], held.at[part], block_sem.at[n]))

    barrier = pltpu.get_barrier_semaphore()
    for n in range(1, grid_rows):
        pl.semaphore_signal(barrier, inc=1, device_id=(row_peer(n), c), device_id_type=MESH)
    for n in range(1, grid_cols):
        pl.semaphore_signal(barrier, inc=1, device_id=(r, col_peer(n)), device_id_type=MESH)

    lane = lax.broadcasted_iota(jnp.int32, (1, slots), 1)
    live = lane < count_ref[0, 0]
    slot_row = slot_row_ref[0]
    slot_col = slot_col_ref[0]
    for base, (keys, partner) in enumerate(
        ((jnp.where(live, slot_row, group_rows), slot_col), (jnp.where(live, slot_col, group_cols), slot_row))
    ):
        for n, found in enumerate(sort_slots(keys, partner, slots)):
            index_v[base * 4 + n : base * 4 + n + 1, :] = found
    index_copy = pltpu.make_async_copy(index_v, index_s, index_sem)
    index_copy.start()

    zeros = jnp.zeros((k, side), F32)
    sums[0, slots] = zeros
    sums[1, slots] = zeros

    start_copy.wait()
    image = start_v[...]

    def share(it, vectors):
        copies = []
        for b in range(owned):
            rounded = vectors[:, b * side : (b + 1) * side].astype(BF16)
            row_vecs[it][c, b] = rounded
            col_vecs[it][r, b] = rounded
        if it == 0:
            pl.semaphore_wait(barrier, grid_rows + grid_cols - 2)
        for n in range(1, grid_rows):
            copies.append(
                pltpu.make_async_remote_copy(
                    col_vecs[it].at[r], col_vecs[it].at[r], col_vec_send.at[it, n], col_vec_recv.at[it, n],
                    device_id=(row_peer(n), c), device_id_type=MESH,
                )
            )
        for n in range(1, grid_cols):
            copies.append(
                pltpu.make_async_remote_copy(
                    row_vecs[it].at[c], row_vecs[it].at[c], row_vec_send.at[it, n], row_vec_recv.at[it, n],
                    device_id=(r, col_peer(n)), device_id_type=MESH,
                )
            )
        for copy in copies:
            copy.start()
        return copies[: grid_rows - 1], copies[grid_rows - 1 :]

    def multiply(which, matrices, vectors, it):
        def some(g, running):
            for u in range(UNROLL):
                s = g * UNROLL + u
                matrix = matrices[index_s[which * 4, s]]
                q = index_s[which * 4 + 1, s]
                vector = vectors[it][q // owned, q % owned]
                product = lax.dot_general(vector, matrix, NN, preferred_element_type=F32)
                running = running * index_s[which * 4 + 2, s].astype(F32) + product
                sums[which, s] = running
            return running

        lax.fori_loop(0, slots // UNROLL, some, zeros)

    def spread(it, which, size, here, staged, landed, send, recv, place):
        copies = []
        for n in range(1, size):
            to = lax.rem(here + n, size)
            for b in range(owned):
                staged[it, to, b] = sums[which, index_s[which * 4 + 3, to * owned + b]].astype(BF16)
            copies.append(
                pltpu.make_async_remote_copy(
                    staged.at[it, to], landed.at[it, here], send.at[it, n], recv.at[it, n],
                    device_id=place(to), device_id_type=MESH,
                )
            )
            copies[-1].start()
        return copies

    def send_gram(it, part, landed, size, here, send, recv, place):
        landed[it, here] = part
        copies = []
        for n in range(1, size):
            copies.append(
                pltpu.make_async_remote_copy(
                    landed.at[it, here], landed.at[it, here], send.at[it, n], recv.at[it, n],
                    device_id=place(lax.rem(here + n, size)), device_id_type=MESH,
                )
            )
            copies[-1].start()
        return copies

    def add_gram(it, copies, landed, size):
        for copy in copies:
            copy.wait()
        total = landed[it, 0]
        for n in range(1, size):
            total = total + landed[it, n]
        return total

    def gram_begin(it, image):
        gram = lax.dot_general(image, image, NT, precision=HIGH, preferred_element_type=F32)
        packed = jnp.concatenate([gram[n * 8 : n * 8 + 8] for n in range(k // 8)], axis=1)
        return send_gram(it, packed, gram_row, grid_rows, r, gram_row_send, gram_row_recv, lambda to: (to, c))

    def gram_middle(it, copies):
        packed = add_gram(it, copies, gram_row, grid_rows)
        return send_gram(it, packed, gram_col, grid_cols, c, gram_col_send, gram_col_recv, lambda to: (r, to))

    def gram_end(it, copies):
        packed = add_gram(it, copies, gram_col, grid_cols)
        gram = jnp.concatenate([packed[:, n * k : n * k + k] for n in range(k // 8)], axis=0)
        return inverse_factor(gram * (1.0 / total_rows))

    def normalise(inverse, image):
        return lax.dot_general(inverse, image, NN, precision=HIGH, preferred_element_type=F32)

    for it in range(ITERS):
        col_copies, row_copies = share(it, image)
        if it == 0:
            for copy in block_copies:
                copy.start()
        if it > 0:
            gram_copies = gram_begin(it - 1, image)
        if it == 0:
            index_copy.wait()
            for n in range(CHUNKS):
                block_copies[n].wait()

                def turn(m, _, n=n):
                    turned[n * per_chunk + m] = held[n * per_chunk + m].T
                    return 0

                lax.fori_loop(0, per_chunk, turn, 0, unroll=True)
        for copy in col_copies:
            copy.wait()
        if it > 0:
            gram_copies = gram_middle(it - 1, gram_copies)
        multiply(0, turned, col_vecs, it)
        row_moves = spread(
            it, 0, grid_cols, c, row_out, row_in, row_out_send, row_out_recv, lambda to: (r, to)
        )
        for copy in row_copies:
            copy.wait()
        multiply(1, held, row_vecs, it)
        col_moves = spread(
            it, 1, grid_rows, r, col_out, col_in, col_out_send, col_out_recv, lambda to: (to, c)
        )
        parts = []
        for b in range(owned):
            part = image[:, b * side : (b + 1) * side]
            weight = weight_ref[pl.ds(b * side, side)].reshape(1, side)
            parts.append(
                part * weight + sums[0, index_s[3, c * owned + b]] + sums[1, index_s[7, r * owned + b]]
            )
        if it > 0:
            inverse = gram_end(it - 1, gram_copies)
        for copy in col_moves:
            copy.wait()
        for n in range(1, grid_rows):
            at = row_peer(n)
            for b in range(owned):
                parts[b] = parts[b] + col_in[it, at, b].astype(F32)
        for copy in row_moves:
            copy.wait()
        for n in range(1, grid_cols):
            at = col_peer(n)
            for b in range(owned):
                parts[b] = parts[b] + row_in[it, at, b].astype(F32)
        image = jnp.concatenate(parts, axis=1)
        if it > 0:
            image = normalise(inverse, image)
    last = ITERS - 1
    inverse = gram_end(last, gram_middle(last, gram_begin(last, image)))
    out_ref[...] = normalise(inverse, image)


def solution(mesh):
    grid_rows, grid_cols = mesh.shape["row"], mesh.shape["col"]

    def shards(start, self_weight, blocks, slot_row, slot_col, slot_count):
        rows, k = start.shape
        slots, side = blocks.shape[2], blocks.shape[3]
        owned = rows // side
        group_rows, group_cols = owned * grid_cols, owned * grid_rows
        total_rows = rows * grid_rows * grid_cols
        any_space = pl.BlockSpec(memory_space=pl.ANY)
        vmem = pl.BlockSpec(memory_space=pltpu.VMEM)
        dma = pltpu.SemaphoreType.DMA
        turned = pl.pallas_call(
            functools.partial(kernel, grid_rows, grid_cols, total_rows),
            out_shape=jax.ShapeDtypeStruct((k, rows), F32),
            in_specs=[any_space, vmem, any_space, vmem, vmem, pl.BlockSpec(memory_space=pltpu.SMEM)],
            out_specs=vmem,
            scratch_shapes=[
                pltpu.VMEM((k, rows), F32),
                pltpu.VMEM((slots, side, side), BF16),
                pltpu.VMEM((slots, side, side), BF16),
                pltpu.VMEM((8, slots), jnp.int32),
                pltpu.SMEM((8, slots), jnp.int32),
                [pltpu.VMEM((grid_cols, owned, k, side), BF16)] * ITERS,
                [pltpu.VMEM((grid_rows, owned, k, side), BF16)] * ITERS,
                pltpu.VMEM((2, slots + 1, k, side), F32),
                pltpu.VMEM((ITERS, grid_cols, owned, k, side), BF16),
                pltpu.VMEM((ITERS, grid_rows, owned, k, side), BF16),
                pltpu.VMEM((ITERS, grid_cols, owned, k, side), BF16),
                pltpu.VMEM((ITERS, grid_rows, owned, k, side), BF16),
                pltpu.VMEM((ITERS, grid_rows, 8, k * k // 8), F32),
                pltpu.VMEM((ITERS, grid_cols, 8, k * k // 8), F32),
                dma,
                dma((CHUNKS,)),
                dma,
            ]
            + [dma((ITERS, n)) for n in (grid_cols, grid_cols, grid_rows, grid_rows)] * 2
            + [dma((ITERS, n)) for n in (grid_rows, grid_rows, grid_cols, grid_cols)],
            compiler_params=pltpu.CompilerParams(
                collective_id=0, has_side_effects=True, vmem_limit_bytes=60 * 2**20
            ),
        )(
            start.T,
            self_weight,
            blocks.reshape(slots, side, side),
            slot_row.reshape(1, 1, slots),
            slot_col.reshape(1, 1, slots),
            slot_count,
        )
        return turned.T

    placed = (
        P(("row", "col"), None),
        P(("row", "col")),
        P("row", "col", None, None, None),
        P("row", "col", None),
        P("row", "col", None),
        P("row", "col"),
    )
    return jax.shard_map(
        shards, mesh=mesh, in_specs=placed, out_specs=P(("row", "col"), None), check_vma=False
    )
```

```python
import functools

import jax
import jax.numpy as jnp
from jax import lax
from jax.experimental import pallas as pl
from jax.experimental.pallas import tpu as pltpu
from jax.sharding import PartitionSpec as P

ITERS = 2
MESH = pl.DeviceIdType.MESH
NT = (((1,), (1,)), ((), ()))
NN = (((1,), (0,)), ((), ()))
HIGH = lax.Precision.HIGHEST
F32 = jnp.float32
BF16 = jnp.bfloat16
UNROLL = 32
HOPS = (2, 3, 1)
Y_FIRST = ((1, 1), (1, 2), (1, 3), (2, 3), (3, 3))
CHUNKS = 16
EARLY_CHUNKS = 8


def sort_slots(keys, partner, spare):
    n = keys.shape[1]
    lane = lax.broadcasted_iota(jnp.int32, (n, n), 1)
    slot = lax.broadcasted_iota(jnp.int32, (n, n), 0)

    def down(row):
        return jnp.broadcast_to(row, (n, n)).T

    def total(mask, value):
        return jnp.sum(jnp.where(mask, value, 0), axis=0, keepdims=True)

    key_down = down(keys)
    key_across = jnp.broadcast_to(keys, (n, n))
    ahead = (key_down < key_across) | ((key_down == key_across) & (slot < lane))
    rank = total(ahead, 1)
    placed = down(rank) == lane
    order = total(placed, slot)
    other = total(placed, down(partner))
    ordered = total(placed, key_down)
    first_lane = lax.broadcasted_iota(jnp.int32, (1, n), 1)
    before = pltpu.roll(ordered, 1, 1)
    keep = jnp.where((first_lane > 0) & (before == ordered), 1, 0)
    last = total(key_down <= lane, 1) - 1
    last = jnp.where(total(key_down == lane, 1) > 0, last, spare)
    return order, other, keep, last


def inverse_factor(gram):
    k = gram.shape[0]
    row = lax.broadcasted_iota(jnp.int32, (k, 2 * k), 0)
    eye = (lax.broadcasted_iota(jnp.int32, (k, k), 0) == lax.broadcasted_iota(jnp.int32, (k, k), 1)).astype(F32)
    work = jnp.concatenate([gram, eye], axis=1)
    for j in range(k):
        scale = lax.rsqrt(work[j : j + 1, j : j + 1])
        pivot = work[j : j + 1, :] * scale
        column = work[:, j : j + 1] * scale
        work = jnp.where(row > j, work - column * pivot, jnp.where(row == j, pivot, work))
    return work[:, k:]


def kernel(
    grid_rows, grid_cols, total_rows,
    start_ref, weight_ref, blocks_ref, slot_row_ref, slot_col_ref, count_ref, out_ref,
    start_v, held, turned, index_v, index_s, row_vecs, col_vecs, sums, row_out, col_out,
    row_in, col_in, gram_row, gram_col,
    start_sem, block_sem, index_sem,
    row_vec_send, row_vec_recv, col_vec_send, col_vec_recv,
    row_out_send, row_out_recv, col_out_send, col_out_recv,
    gram_row_send, gram_row_recv, gram_col_send, gram_col_recv,
):
    r = lax.axis_index("row")
    c = lax.axis_index("col")
    slots, side, _ = held.shape
    owned = row_in.shape[2]
    k = start_v.shape[0]
    group_rows = owned * grid_cols
    group_cols = owned * grid_rows
    per_chunk = slots // CHUNKS

    def row_peer(n):
        return lax.rem(r + n, grid_rows)

    def col_peer(n):
        return lax.rem(c + n, grid_cols)

    def shifted(here, by, size):
        return lax.rem(here + by, size)

    other_core = r + 1 - 2 * lax.rem(r, 2)

    def along_x(n):
        x = lax.rem(c, 4)
        return c - x + lax.rem(x + n, 4)

    start_copy = pltpu.make_async_copy(start_ref, start_v, start_sem)
    start_copy.start()
    block_copies = []
    for n in range(CHUNKS):
        part = pl.ds(n * per_chunk, per_chunk)
        block_copies.append(pltpu.make_async_copy(blocks_ref.at[part], held.at[part], block_sem.at[n]))

    barrier = pltpu.get_barrier_semaphore()
    near = [(other_core, c)]
    for n in HOPS:
        near += [(shifted(r, n * 2, grid_rows), c), (r, shifted(c, n * 4, grid_cols)), (r, along_x(n))]
    for place in near:
        pl.semaphore_signal(barrier, inc=1, device_id=place, device_id_type=MESH)

    lane = lax.broadcasted_iota(jnp.int32, (1, slots), 1)
    live = lane < count_ref[0, 0]
    slot_row = slot_row_ref[0]
    slot_col = slot_col_ref[0]
    for base, (keys, partner) in enumerate(
        ((jnp.where(live, slot_row, group_rows), slot_col), (jnp.where(live, slot_col, group_cols), slot_row))
    ):
        for n, found in enumerate(sort_slots(keys, partner, slots)):
            index_v[base * 4 + n : base * 4 + n + 1, :] = found
    index_copy = pltpu.make_async_copy(index_v, index_s, index_sem)
    index_copy.start()

    zeros = jnp.zeros((k, side), F32)
    sums[0, slots] = zeros
    sums[1, slots] = zeros

    start_copy.wait()
    image = start_v[...]

    def share(it, vectors):
        for b in range(owned):
            rounded = vectors[:, b * side : (b + 1) * side].astype(BF16)
            row_vecs[it][c, b] = rounded
            col_vecs[it][r, b] = rounded
        if it == 0:
            pl.semaphore_wait(barrier, len(near))
        sent = {}
        for n in HOPS:
            send_col(it, sent, 2 * n, r, shifted(r, n * 2, grid_rows))
            send_row(it, sent, 4 * n, c, shifted(c, n * 4, grid_cols))
            send_row(it, sent, n, c, along_x(n))
        send_col(it, sent, 1, r, other_core)
        return sent

    def send_col(it, sent, n, source, to):
        sent["col", n] = pltpu.make_async_remote_copy(
            col_vecs[it].at[source], col_vecs[it].at[source], col_vec_send.at[it, n], col_vec_recv.at[it, n],
            device_id=(to, c), device_id_type=MESH,
        )
        sent["col", n].start()

    def send_row(it, sent, n, source, to):
        sent["row", n] = pltpu.make_async_remote_copy(
            row_vecs[it].at[source], row_vecs[it].at[source], row_vec_send.at[it, n], row_vec_recv.at[it, n],
            device_id=(r, to), device_id_type=MESH,
        )
        sent["row", n].start()

    def pass_on(it, sent):
        for n in reversed(HOPS):
            sent["col", 2 * n].wait_recv()
            send_col(it, sent, 2 * n + 1, shifted(r, grid_rows - n * 2, grid_rows), other_core)
            sent["row", 4 * n].wait_recv()
            for m in HOPS:
                if (n, m) in Y_FIRST:
                    send_row(it, sent, 4 * n + m, shifted(c, grid_cols - n * 4, grid_cols), along_x(m))
            sent["row", n].wait_recv()
            for m in HOPS:
                if (m, n) not in Y_FIRST:
                    send_row(it, sent, 4 * m + n, along_x(4 - n), shifted(c, m * 4, grid_cols))

    def finish(sent, axis):
        arrived = 2 if axis == "col" else 4
        for n in range(1, grid_rows if axis == "col" else grid_cols):
            passed = n % arrived == 0 or (axis == "row" and n < arrived)
            sent[axis, n].wait_send() if passed else sent[axis, n].wait()

    def multiply(which, matrices, vectors, it):
        def some(g, running):
            for u in range(UNROLL):
                s = g * UNROLL + u
                matrix = matrices[index_s[which * 4, s]]
                q = index_s[which * 4 + 1, s]
                vector = vectors[it][q // owned, q % owned]
                product = lax.dot_general(vector, matrix, NN, preferred_element_type=F32)
                running = running * index_s[which * 4 + 2, s].astype(F32) + product
                sums[which, s] = running
            return running

        lax.fori_loop(0, slots // UNROLL, some, zeros)

    def spread(it, which, size, here, staged, landed, send, recv, place):
        copies = []
        for n in range(1, size):
            to = lax.rem(here + n, size)
            for b in range(owned):
                staged[it, to, b] = sums[which, index_s[which * 4 + 3, to * owned + b]].astype(BF16)
            copies.append(
                pltpu.make_async_remote_copy(
                    staged.at[it, to], landed.at[it, here], send.at[it, n], recv.at[it, n],
                    device_id=place(to), device_id_type=MESH,
                )
            )
            copies[-1].start()
        return copies

    def send_gram(it, part, landed, size, here, send, recv, place):
        landed[it, here] = part
        copies = []
        for n in range(1, size):
            copies.append(
                pltpu.make_async_remote_copy(
                    landed.at[it, here], landed.at[it, here], send.at[it, n], recv.at[it, n],
                    device_id=place(lax.rem(here + n, size)), device_id_type=MESH,
                )
            )
            copies[-1].start()
        return copies

    def add_gram(it, copies, landed, size):
        for copy in copies:
            copy.wait()
        total = landed[it, 0]
        for n in range(1, size):
            total = total + landed[it, n]
        return total

    def gram_begin(it, image):
        gram = lax.dot_general(image, image, NT, precision=HIGH, preferred_element_type=F32)
        packed = jnp.concatenate([gram[n * 8 : n * 8 + 8] for n in range(k // 8)], axis=1)
        return send_gram(it, packed, gram_row, grid_rows, r, gram_row_send, gram_row_recv, lambda to: (to, c))

    def gram_middle(it, copies):
        packed = add_gram(it, copies, gram_row, grid_rows)
        return send_gram(it, packed, gram_col, grid_cols, c, gram_col_send, gram_col_recv, lambda to: (r, to))

    def gram_end(it, copies):
        packed = add_gram(it, copies, gram_col, grid_cols)
        gram = jnp.concatenate([packed[:, n * k : n * k + k] for n in range(k // 8)], axis=0)
        return inverse_factor(gram * (1.0 / total_rows))

    def normalise(inverse, image):
        return lax.dot_general(inverse, image, NN, precision=HIGH, preferred_element_type=F32)

    def turn_chunks(first, end):
        for n in range(first, end):
            block_copies[n].wait()

            def turn(m, _, n=n):
                turned[n * per_chunk + m] = held[n * per_chunk + m].T
                return 0

            lax.fori_loop(0, per_chunk, turn, 0, unroll=True)

    for it in range(ITERS):
        sent = share(it, image)
        if it == 0:
            for copy in block_copies:
                copy.start()
        if it > 0:
            gram_copies = gram_begin(it - 1, image)
        if it == 0:
            turn_chunks(0, EARLY_CHUNKS)
        pass_on(it, sent)
        if it == 0:
            turn_chunks(EARLY_CHUNKS, CHUNKS)
            index_copy.wait()
        finish(sent, "col")
        if it > 0:
            gram_copies = gram_middle(it - 1, gram_copies)
        multiply(0, turned, col_vecs, it)
        row_moves = spread(
            it, 0, grid_cols, c, row_out, row_in, row_out_send, row_out_recv, lambda to: (r, to)
        )
        finish(sent, "row")
        multiply(1, held, row_vecs, it)
        col_moves = spread(
            it, 1, grid_rows, r, col_out, col_in, col_out_send, col_out_recv, lambda to: (to, c)
        )
        parts = []
        for b in range(owned):
            part = image[:, b * side : (b + 1) * side]
            weight = weight_ref[pl.ds(b * side, side)].reshape(1, side)
            parts.append(
                part * weight + sums[0, index_s[3, c * owned + b]] + sums[1, index_s[7, r * owned + b]]
            )
        if it > 0:
            inverse = gram_end(it - 1, gram_copies)
        for copy in col_moves:
            copy.wait()
        for n in range(1, grid_rows):
            at = row_peer(n)
            for b in range(owned):
                parts[b] = parts[b] + col_in[it, at, b].astype(F32)
        for copy in row_moves:
            copy.wait()
        for n in range(1, grid_cols):
            at = col_peer(n)
            for b in range(owned):
                parts[b] = parts[b] + row_in[it, at, b].astype(F32)
        image = jnp.concatenate(parts, axis=1)
        if it > 0:
            image = normalise(inverse, image)
    last = ITERS - 1
    inverse = gram_end(last, gram_middle(last, gram_begin(last, image)))
    out_ref[...] = normalise(inverse, image)


def solution(mesh):
    grid_rows, grid_cols = mesh.shape["row"], mesh.shape["col"]

    def shards(start, self_weight, blocks, slot_row, slot_col, slot_count):
        rows, k = start.shape
        slots, side = blocks.shape[2], blocks.shape[3]
        owned = rows // side
        group_rows, group_cols = owned * grid_cols, owned * grid_rows
        total_rows = rows * grid_rows * grid_cols
        any_space = pl.BlockSpec(memory_space=pl.ANY)
        vmem = pl.BlockSpec(memory_space=pltpu.VMEM)
        dma = pltpu.SemaphoreType.DMA
        turned = pl.pallas_call(
            functools.partial(kernel, grid_rows, grid_cols, total_rows),
            out_shape=jax.ShapeDtypeStruct((k, rows), F32),
            in_specs=[any_space, vmem, any_space, vmem, vmem, pl.BlockSpec(memory_space=pltpu.SMEM)],
            out_specs=vmem,
            scratch_shapes=[
                pltpu.VMEM((k, rows), F32),
                pltpu.VMEM((slots, side, side), BF16),
                pltpu.VMEM((slots, side, side), BF16),
                pltpu.VMEM((8, slots), jnp.int32),
                pltpu.SMEM((8, slots), jnp.int32),
                [pltpu.VMEM((grid_cols, owned, k, side), BF16)] * ITERS,
                [pltpu.VMEM((grid_rows, owned, k, side), BF16)] * ITERS,
                pltpu.VMEM((2, slots + 1, k, side), F32),
                pltpu.VMEM((ITERS, grid_cols, owned, k, side), BF16),
                pltpu.VMEM((ITERS, grid_rows, owned, k, side), BF16),
                pltpu.VMEM((ITERS, grid_cols, owned, k, side), BF16),
                pltpu.VMEM((ITERS, grid_rows, owned, k, side), BF16),
                pltpu.VMEM((ITERS, grid_rows, 8, k * k // 8), F32),
                pltpu.VMEM((ITERS, grid_cols, 8, k * k // 8), F32),
                dma,
                dma((CHUNKS,)),
                dma,
            ]
            + [dma((ITERS, n)) for n in (grid_cols, grid_cols, grid_rows, grid_rows)] * 2
            + [dma((ITERS, n)) for n in (grid_rows, grid_rows, grid_cols, grid_cols)],
            compiler_params=pltpu.CompilerParams(
                collective_id=0, has_side_effects=True, vmem_limit_bytes=60 * 2**20
            ),
        )(
            start.T,
            self_weight,
            blocks.reshape(slots, side, side),
            slot_row.reshape(1, 1, slots),
            slot_col.reshape(1, 1, slots),
            slot_count,
        )
        return turned.T

    placed = (
        P(("row", "col"), None),
        P(("row", "col")),
        P("row", "col", None, None, None),
        P("row", "col", None),
        P("row", "col", None),
        P("row", "col"),
    )
    return jax.shard_map(
        shards, mesh=mesh, in_specs=placed, out_specs=P(("row", "col"), None), check_vma=False
    )
```

```python
import functools

import jax
import jax.numpy as jnp
from jax import lax
from jax.experimental import pallas as pl
from jax.experimental.pallas import tpu as pltpu
from jax.sharding import PartitionSpec as P

ITERS = 2
MESH = pl.DeviceIdType.MESH
NT = (((1,), (1,)), ((), ()))
NN = (((1,), (0,)), ((), ()))
HIGH = lax.Precision.HIGHEST
F32 = jnp.float32
BF16 = jnp.bfloat16
UNROLL = 128
PIVOTS = 8
HOPS = (2, 3, 1)
Y_FIRST = ((1, 1), (1, 2), (1, 3), (2, 3), (3, 3))
CHUNKS = 16
EARLY_CHUNKS = 8


def sort_slots(keys, partner, spare):
    n = keys.shape[1]
    lane = lax.broadcasted_iota(jnp.int32, (n, n), 1)
    slot = lax.broadcasted_iota(jnp.int32, (n, n), 0)

    def down(row):
        return jnp.broadcast_to(row, (n, n)).T

    def total(mask, value):
        return jnp.sum(jnp.where(mask, value, 0), axis=0, keepdims=True)

    key_down = down(keys)
    key_across = jnp.broadcast_to(keys, (n, n))
    ahead = (key_down < key_across) | ((key_down == key_across) & (slot < lane))
    rank = total(ahead, 1)
    placed = down(rank) == lane
    order = total(placed, slot)
    other = total(placed, down(partner))
    ordered = total(placed, key_down)
    first_lane = lax.broadcasted_iota(jnp.int32, (1, n), 1)
    before = pltpu.roll(ordered, 1, 1)
    keep = jnp.where((first_lane > 0) & (before == ordered), 1, 0)
    last = total(key_down <= lane, 1) - 1
    last = jnp.where(total(key_down == lane, 1) > 0, last, spare)
    return order, other, keep, last


def inverse_factor(gram):
    k = gram.shape[0]
    eye = (lax.broadcasted_iota(jnp.int32, (k, k), 0) == lax.broadcasted_iota(jnp.int32, (k, k), 1)).astype(F32)
    work = jnp.concatenate([gram, eye], axis=1)
    found = []
    for j in range(0, k, PIVOTS):
        rows = [work[j + n : j + n + 1, :] for n in range(PIVOTS)]
        columns = [jnp.broadcast_to(work[:, j + n : j + n + 1], (k, 2 * k)) for n in range(PIVOTS)]
        corner = [
            [None] * n + [jnp.broadcast_to(rows[n][:, j + m : j + m + 1], (1, 2 * k)) for m in range(n, PIVOTS)]
            for n in range(PIVOTS)
        ]
        factors, spread = {}, []
        for n in range(PIVOTS):
            over = 1.0 / corner[n][n]
            for t in range(n + 1, PIVOTS):
                factors[n, t] = corner[n][t] * over
            for t in range(n + 1, PIVOTS):
                rows[t] = rows[t] - factors[n, t] * rows[n]
                for m in range(t, PIVOTS):
                    corner[t][m] = corner[t][m] - factors[n, t] * corner[n][m]
            spread.append(rows[n] * over)
            found.append(rows[n][:, k:] * lax.rsqrt(corner[n][n][:, k:]))
        for n in reversed(range(PIVOTS)):
            for t in range(n + 1, PIVOTS):
                spread[n] = spread[n] - factors[n, t] * spread[t]
        for n in range(PIVOTS):
            work = work - columns[n] * spread[n]
    return jnp.concatenate(found, axis=0)


def kernel(
    grid_rows, grid_cols, total_rows,
    start_ref, weight_ref, blocks_ref, slot_row_ref, slot_col_ref, count_ref, out_ref,
    start_v, held, turned, index_v, index_s, row_vecs, col_vecs, sums, row_out, col_out,
    row_in, col_in, gram_row, gram_col,
    start_sem, block_sem, index_sem,
    row_vec_send, row_vec_recv, col_vec_send, col_vec_recv,
    row_out_send, row_out_recv, col_out_send, col_out_recv,
    gram_row_send, gram_row_recv, gram_col_send, gram_col_recv,
):
    r = lax.axis_index("row")
    c = lax.axis_index("col")
    slots, side, _ = held.shape
    owned = row_in.shape[2]
    k = start_v.shape[0]
    group_rows = owned * grid_cols
    group_cols = owned * grid_rows
    per_chunk = slots // CHUNKS

    def row_peer(n):
        return lax.rem(r + n, grid_rows)

    def col_peer(n):
        return lax.rem(c + n, grid_cols)

    def shifted(here, by, size):
        return lax.rem(here + by, size)

    other_core = r + 1 - 2 * lax.rem(r, 2)

    def along_x(n):
        x = lax.rem(c, 4)
        return c - x + lax.rem(x + n, 4)

    start_copy = pltpu.make_async_copy(start_ref, start_v, start_sem)
    start_copy.start()
    block_copies = []
    for n in range(CHUNKS):
        part = pl.ds(n * per_chunk, per_chunk)
        block_copies.append(pltpu.make_async_copy(blocks_ref.at[part], held.at[part], block_sem.at[n]))

    barrier = pltpu.get_barrier_semaphore()
    near = [(other_core, c)]
    for n in HOPS:
        near += [(shifted(r, n * 2, grid_rows), c), (r, shifted(c, n * 4, grid_cols)), (r, along_x(n))]
    for place in near:
        pl.semaphore_signal(barrier, inc=1, device_id=place, device_id_type=MESH)

    lane = lax.broadcasted_iota(jnp.int32, (1, slots), 1)
    live = lane < count_ref[0, 0]
    slot_row = slot_row_ref[0]
    slot_col = slot_col_ref[0]
    for base, (keys, partner) in enumerate(
        ((jnp.where(live, slot_row, group_rows), slot_col), (jnp.where(live, slot_col, group_cols), slot_row))
    ):
        for n, found in enumerate(sort_slots(keys, partner, slots)):
            index_v[base * 4 + n : base * 4 + n + 1, :] = found
    index_copy = pltpu.make_async_copy(index_v, index_s, index_sem)
    index_copy.start()

    zeros = jnp.zeros((k, side), F32)
    sums[0, slots] = zeros
    sums[1, slots] = zeros

    start_copy.wait()
    image = start_v[...]

    def share(it, vectors):
        for b in range(owned):
            rounded = vectors[:, b * side : (b + 1) * side].astype(BF16)
            row_vecs[it][c, b] = rounded
            col_vecs[it][r, b] = rounded
        if it == 0:
            pl.semaphore_wait(barrier, len(near))
        sent = {}
        for n in HOPS:
            send_col(it, sent, 2 * n, r, shifted(r, n * 2, grid_rows))
            send_row(it, sent, 4 * n, c, shifted(c, n * 4, grid_cols))
            send_row(it, sent, n, c, along_x(n))
        send_col(it, sent, 1, r, other_core)
        return sent

    def send_col(it, sent, n, source, to):
        sent["col", n] = pltpu.make_async_remote_copy(
            col_vecs[it].at[source], col_vecs[it].at[source], col_vec_send.at[it, n], col_vec_recv.at[it, n],
            device_id=(to, c), device_id_type=MESH,
        )
        sent["col", n].start()

    def send_row(it, sent, n, source, to):
        sent["row", n] = pltpu.make_async_remote_copy(
            row_vecs[it].at[source], row_vecs[it].at[source], row_vec_send.at[it, n], row_vec_recv.at[it, n],
            device_id=(r, to), device_id_type=MESH,
        )
        sent["row", n].start()

    def pass_on(it, sent):
        for n in reversed(HOPS):
            sent["col", 2 * n].wait_recv()
            send_col(it, sent, 2 * n + 1, shifted(r, grid_rows - n * 2, grid_rows), other_core)
            sent["row", 4 * n].wait_recv()
            for m in HOPS:
                if (n, m) in Y_FIRST:
                    send_row(it, sent, 4 * n + m, shifted(c, grid_cols - n * 4, grid_cols), along_x(m))
            sent["row", n].wait_recv()
            for m in HOPS:
                if (m, n) not in Y_FIRST:
                    send_row(it, sent, 4 * m + n, along_x(4 - n), shifted(c, m * 4, grid_cols))

    def finish(sent, axis):
        arrived = 2 if axis == "col" else 4
        for n in range(1, grid_rows if axis == "col" else grid_cols):
            passed = n % arrived == 0 or (axis == "row" and n < arrived)
            sent[axis, n].wait_send() if passed else sent[axis, n].wait()

    def multiply(which, matrices, vectors, it):
        def some(g, running):
            for u in range(UNROLL):
                s = g * UNROLL + u
                matrix = matrices[index_s[which * 4, s]]
                q = index_s[which * 4 + 1, s]
                vector = vectors[it][q // owned, q % owned]
                product = lax.dot_general(vector, matrix, NN, preferred_element_type=F32)
                running = running * index_s[which * 4 + 2, s].astype(F32) + product
                sums[which, s] = running
            return running

        lax.fori_loop(0, slots // UNROLL, some, zeros)

    def spread(it, which, size, here, staged, landed, send, recv, place):
        copies = []
        for n in range(1, size):
            to = lax.rem(here + n, size)
            for b in range(owned):
                staged[it, to, b] = sums[which, index_s[which * 4 + 3, to * owned + b]].astype(BF16)
            copies.append(
                pltpu.make_async_remote_copy(
                    staged.at[it, to], landed.at[it, here], send.at[it, n], recv.at[it, n],
                    device_id=place(to), device_id_type=MESH,
                )
            )
            copies[-1].start()
        return copies

    def send_gram(it, part, landed, size, here, send, recv, place):
        landed[it, here] = part
        copies = []
        for n in range(1, size):
            copies.append(
                pltpu.make_async_remote_copy(
                    landed.at[it, here], landed.at[it, here], send.at[it, n], recv.at[it, n],
                    device_id=place(lax.rem(here + n, size)), device_id_type=MESH,
                )
            )
            copies[-1].start()
        return copies

    def add_gram(it, copies, landed, size):
        for copy in copies:
            copy.wait()
        total = landed[it, 0]
        for n in range(1, size):
            total = total + landed[it, n]
        return total

    def gram_begin(it, image):
        gram = lax.dot_general(image, image, NT, precision=HIGH, preferred_element_type=F32)
        packed = jnp.concatenate([gram[n * 8 : n * 8 + 8] for n in range(k // 8)], axis=1)
        return send_gram(it, packed, gram_row, grid_rows, r, gram_row_send, gram_row_recv, lambda to: (to, c))

    def gram_middle(it, copies):
        packed = add_gram(it, copies, gram_row, grid_rows)
        return send_gram(it, packed, gram_col, grid_cols, c, gram_col_send, gram_col_recv, lambda to: (r, to))

    def gram_end(it, copies):
        packed = add_gram(it, copies, gram_col, grid_cols)
        gram = jnp.concatenate([packed[:, n * k : n * k + k] for n in range(k // 8)], axis=0)
        return inverse_factor(gram * (1.0 / total_rows))

    def normalise(inverse, image):
        return lax.dot_general(inverse, image, NN, precision=HIGH, preferred_element_type=F32)

    def turn_chunks(first, end):
        for n in range(first, end):
            block_copies[n].wait()

            def turn(m, _, n=n):
                turned[n * per_chunk + m] = held[n * per_chunk + m].T
                return 0

            lax.fori_loop(0, per_chunk, turn, 0, unroll=True)

    for it in range(ITERS):
        sent = share(it, image)
        if it == 0:
            for copy in block_copies:
                copy.start()
        if it > 0:
            gram_copies = gram_begin(it - 1, image)
        if it == 0:
            turn_chunks(0, EARLY_CHUNKS)
        pass_on(it, sent)
        if it == 0:
            turn_chunks(EARLY_CHUNKS, CHUNKS)
            index_copy.wait()
        finish(sent, "col")
        if it > 0:
            gram_copies = gram_middle(it - 1, gram_copies)
        multiply(0, turned, col_vecs, it)
        row_moves = spread(
            it, 0, grid_cols, c, row_out, row_in, row_out_send, row_out_recv, lambda to: (r, to)
        )
        finish(sent, "row")
        multiply(1, held, row_vecs, it)
        col_moves = spread(
            it, 1, grid_rows, r, col_out, col_in, col_out_send, col_out_recv, lambda to: (to, c)
        )
        parts = []
        for b in range(owned):
            part = image[:, b * side : (b + 1) * side]
            weight = weight_ref[pl.ds(b * side, side)].reshape(1, side)
            parts.append(
                part * weight + sums[0, index_s[3, c * owned + b]] + sums[1, index_s[7, r * owned + b]]
            )
        if it > 0:
            inverse = gram_end(it - 1, gram_copies)
        for copy in col_moves:
            copy.wait()
        for n in range(1, grid_rows):
            at = row_peer(n)
            for b in range(owned):
                parts[b] = parts[b] + col_in[it, at, b].astype(F32)
        for copy in row_moves:
            copy.wait()
        for n in range(1, grid_cols):
            at = col_peer(n)
            for b in range(owned):
                parts[b] = parts[b] + row_in[it, at, b].astype(F32)
        image = jnp.concatenate(parts, axis=1)
        if it > 0:
            image = normalise(inverse, image)
    last = ITERS - 1
    inverse = gram_end(last, gram_middle(last, gram_begin(last, image)))
    out_ref[...] = normalise(inverse, image)


def solution(mesh):
    grid_rows, grid_cols = mesh.shape["row"], mesh.shape["col"]

    def shards(start, self_weight, blocks, slot_row, slot_col, slot_count):
        rows, k = start.shape
        slots, side = blocks.shape[2], blocks.shape[3]
        owned = rows // side
        group_rows, group_cols = owned * grid_cols, owned * grid_rows
        total_rows = rows * grid_rows * grid_cols
        any_space = pl.BlockSpec(memory_space=pl.ANY)
        vmem = pl.BlockSpec(memory_space=pltpu.VMEM)
        dma = pltpu.SemaphoreType.DMA
        turned = pl.pallas_call(
            functools.partial(kernel, grid_rows, grid_cols, total_rows),
            out_shape=jax.ShapeDtypeStruct((k, rows), F32),
            in_specs=[any_space, vmem, any_space, vmem, vmem, pl.BlockSpec(memory_space=pltpu.SMEM)],
            out_specs=vmem,
            scratch_shapes=[
                pltpu.VMEM((k, rows), F32),
                pltpu.VMEM((slots, side, side), BF16),
                pltpu.VMEM((slots, side, side), BF16),
                pltpu.VMEM((8, slots), jnp.int32),
                pltpu.SMEM((8, slots), jnp.int32),
                [pltpu.VMEM((grid_cols, owned, k, side), BF16)] * ITERS,
                [pltpu.VMEM((grid_rows, owned, k, side), BF16)] * ITERS,
                pltpu.VMEM((2, slots + 1, k, side), F32),
                pltpu.VMEM((ITERS, grid_cols, owned, k, side), BF16),
                pltpu.VMEM((ITERS, grid_rows, owned, k, side), BF16),
                pltpu.VMEM((ITERS, grid_cols, owned, k, side), BF16),
                pltpu.VMEM((ITERS, grid_rows, owned, k, side), BF16),
                pltpu.VMEM((ITERS, grid_rows, 8, k * k // 8), F32),
                pltpu.VMEM((ITERS, grid_cols, 8, k * k // 8), F32),
                dma,
                dma((CHUNKS,)),
                dma,
            ]
            + [dma((ITERS, n)) for n in (grid_cols, grid_cols, grid_rows, grid_rows)] * 2
            + [dma((ITERS, n)) for n in (grid_rows, grid_rows, grid_cols, grid_cols)],
            compiler_params=pltpu.CompilerParams(
                collective_id=0, has_side_effects=True, vmem_limit_bytes=60 * 2**20
            ),
        )(
            start.T,
            self_weight,
            blocks.reshape(slots, side, side),
            slot_row.reshape(1, 1, slots),
            slot_col.reshape(1, 1, slots),
            slot_count,
        )
        return turned.T

    placed = (
        P(("row", "col"), None),
        P(("row", "col")),
        P("row", "col", None, None, None),
        P("row", "col", None),
        P("row", "col", None),
        P("row", "col"),
    )
    return jax.shard_map(
        shards, mesh=mesh, in_specs=placed, out_specs=P(("row", "col"), None), check_vma=False
    )
```

```python
import functools

import jax
import jax.numpy as jnp
from jax import lax
from jax.experimental import pallas as pl
from jax.experimental.pallas import tpu as pltpu
from jax.sharding import PartitionSpec as P

ITERS = 2
MESH = pl.DeviceIdType.MESH
NT = (((1,), (1,)), ((), ()))
NN = (((1,), (0,)), ((), ()))
HIGH = lax.Precision.HIGHEST
F32 = jnp.float32
BF16 = jnp.bfloat16
UNROLL = 128
PIVOTS = 8
HOPS = (2, 3, 1)
Y_FIRST = ((1, 1), (1, 2), (1, 3), (2, 3), (3, 3))
CHUNKS = 16
EARLY_CHUNKS = 8


def sort_slots(keys, partner, spare):
    n = keys.shape[1]
    lane = lax.broadcasted_iota(jnp.int32, (n, n), 1)
    slot = lax.broadcasted_iota(jnp.int32, (n, n), 0)

    def down(row):
        return jnp.broadcast_to(row, (n, n)).T

    def total(mask, value):
        return jnp.sum(jnp.where(mask, value, 0), axis=0, keepdims=True)

    key_down = down(keys)
    key_across = jnp.broadcast_to(keys, (n, n))
    ahead = (key_down < key_across) | ((key_down == key_across) & (slot < lane))
    rank = total(ahead, 1)
    placed = down(rank) == lane
    order = total(placed, slot)
    other = total(placed, down(partner))
    ordered = total(placed, key_down)
    first_lane = lax.broadcasted_iota(jnp.int32, (1, n), 1)
    before = pltpu.roll(ordered, 1, 1)
    keep = jnp.where((first_lane > 0) & (before == ordered), 1, 0)
    last = total(key_down <= lane, 1) - 1
    last = jnp.where(total(key_down == lane, 1) > 0, last, spare)
    return order, other, keep, last


def inverse_factor(gram):
    k = gram.shape[0]
    eye = (lax.broadcasted_iota(jnp.int32, (k, k), 0) == lax.broadcasted_iota(jnp.int32, (k, k), 1)).astype(F32)
    work = jnp.concatenate([gram, eye], axis=1)
    found = []
    for j in range(0, k, PIVOTS):
        rows = [work[j + n : j + n + 1, :] for n in range(PIVOTS)]
        columns = [jnp.broadcast_to(work[:, j + n : j + n + 1], (k, 2 * k)) for n in range(PIVOTS)]
        corner = [
            [None] * n + [jnp.broadcast_to(rows[n][:, j + m : j + m + 1], (1, 2 * k)) for m in range(n, PIVOTS)]
            for n in range(PIVOTS)
        ]
        factors, spread = {}, []
        for n in range(PIVOTS):
            over = 1.0 / corner[n][n]
            for t in range(n + 1, PIVOTS):
                factors[n, t] = corner[n][t] * over
            for t in range(n + 1, PIVOTS):
                rows[t] = rows[t] - factors[n, t] * rows[n]
                for m in range(t, PIVOTS):
                    corner[t][m] = corner[t][m] - factors[n, t] * corner[n][m]
            spread.append(rows[n] * over)
            found.append(rows[n][:, k:] * lax.rsqrt(corner[n][n][:, k:]))
        for n in reversed(range(PIVOTS)):
            for t in range(n + 1, PIVOTS):
                spread[n] = spread[n] - factors[n, t] * spread[t]
        for n in range(PIVOTS):
            work = work - columns[n] * spread[n]
    return jnp.concatenate(found, axis=0)


def kernel(
    grid_rows, grid_cols, total_rows,
    start_ref, weight_ref, blocks_ref, slot_row_ref, slot_col_ref, count_ref, out_ref,
    start_v, held, turned, index_v, index_s, row_vecs, col_vecs, sums, row_out, col_out,
    row_in, col_in, gram_row, gram_col,
    start_sem, block_sem, index_sem,
    row_vec_send, row_vec_recv, col_vec_send, col_vec_recv,
    row_out_send, row_out_recv, col_out_send, col_out_recv,
    gram_row_send, gram_row_recv, gram_col_send, gram_col_recv,
):
    r = lax.axis_index("row")
    c = lax.axis_index("col")
    slots, side, _ = held.shape
    owned = row_in.shape[2]
    k = start_v.shape[0]
    group_rows = owned * grid_cols
    group_cols = owned * grid_rows
    per_chunk = slots // CHUNKS

    def row_peer(n):
        return lax.rem(r + n, grid_rows)

    def col_peer(n):
        return lax.rem(c + n, grid_cols)

    def shifted(here, by, size):
        return lax.rem(here + by, size)

    other_core = r + 1 - 2 * lax.rem(r, 2)

    def along_x(n):
        x = lax.rem(c, 4)
        return c - x + lax.rem(x + n, 4)

    start_copy = pltpu.make_async_copy(start_ref, start_v, start_sem)
    start_copy.start()
    block_copies = []
    for n in range(CHUNKS):
        part = pl.ds(n * per_chunk, per_chunk)
        block_copies.append(pltpu.make_async_copy(blocks_ref.at[part], held.at[part], block_sem.at[n]))

    barrier = pltpu.get_barrier_semaphore()
    near = [(other_core, c)]
    for n in HOPS:
        near += [(shifted(r, n * 2, grid_rows), c), (r, shifted(c, n * 4, grid_cols)), (r, along_x(n))]
    for place in near:
        pl.semaphore_signal(barrier, inc=1, device_id=place, device_id_type=MESH)

    lane = lax.broadcasted_iota(jnp.int32, (1, slots), 1)
    live = lane < count_ref[0, 0]
    slot_row = slot_row_ref[0]
    slot_col = slot_col_ref[0]
    for base, (keys, partner) in enumerate(
        ((jnp.where(live, slot_row, group_rows), slot_col), (jnp.where(live, slot_col, group_cols), slot_row))
    ):
        for n, found in enumerate(sort_slots(keys, partner, slots)):
            index_v[base * 4 + n : base * 4 + n + 1, :] = found
    index_copy = pltpu.make_async_copy(index_v, index_s, index_sem)
    index_copy.start()

    zeros = jnp.zeros((k, side), F32)
    sums[0, slots] = zeros
    sums[1, slots] = zeros

    start_copy.wait()
    image = start_v[...]

    def share(it, vectors):
        for b in range(owned):
            rounded = vectors[:, b * side : (b + 1) * side].astype(BF16)
            row_vecs[it][c, b] = rounded
            col_vecs[it][r, b] = rounded
        if it == 0:
            pl.semaphore_wait(barrier, len(near))
        sent = {}
        for n in HOPS:
            send_col(it, sent, 2 * n, r, shifted(r, n * 2, grid_rows))
            send_row(it, sent, 4 * n, c, shifted(c, n * 4, grid_cols))
            send_row(it, sent, n, c, along_x(n))
        send_col(it, sent, 1, r, other_core)
        return sent

    def send_col(it, sent, n, source, to):
        sent["col", n] = pltpu.make_async_remote_copy(
            col_vecs[it].at[source], col_vecs[it].at[source], col_vec_send.at[it, n], col_vec_recv.at[it, n],
            device_id=(to, c), device_id_type=MESH,
        )
        sent["col", n].start()

    def send_row(it, sent, n, source, to):
        sent["row", n] = pltpu.make_async_remote_copy(
            row_vecs[it].at[source], row_vecs[it].at[source], row_vec_send.at[it, n], row_vec_recv.at[it, n],
            device_id=(r, to), device_id_type=MESH,
        )
        sent["row", n].start()

    def pass_on(it, sent):
        for n in reversed(HOPS):
            sent["col", 2 * n].wait_recv()
            send_col(it, sent, 2 * n + 1, shifted(r, grid_rows - n * 2, grid_rows), other_core)
        for n in reversed(HOPS):
            sent["row", 4 * n].wait_recv()
            for m in HOPS:
                if (n, m) in Y_FIRST:
                    send_row(it, sent, 4 * n + m, shifted(c, grid_cols - n * 4, grid_cols), along_x(m))
            sent["row", n].wait_recv()
            for m in HOPS:
                if (m, n) not in Y_FIRST:
                    send_row(it, sent, 4 * m + n, along_x(4 - n), shifted(c, m * 4, grid_cols))

    def finish(sent, axis):
        arrived = 2 if axis == "col" else 4
        for n in range(1, grid_rows if axis == "col" else grid_cols):
            passed = n % arrived == 0 or (axis == "row" and n < arrived)
            sent[axis, n].wait_send() if passed else sent[axis, n].wait()

    def multiply(which, matrices, vectors, it):
        def some(g, running):
            for u in range(UNROLL):
                s = g * UNROLL + u
                matrix = matrices[index_s[which * 4, s]]
                q = index_s[which * 4 + 1, s]
                vector = vectors[it][q // owned, q % owned]
                product = lax.dot_general(vector, matrix, NN, preferred_element_type=F32)
                running = running * index_s[which * 4 + 2, s].astype(F32) + product
                sums[which, s] = running
            return running

        lax.fori_loop(0, slots // UNROLL, some, zeros)

    def spread(it, which, size, here, staged, landed, send, recv, place):
        copies = []
        for n in range(1, size):
            to = lax.rem(here + n, size)
            for b in range(owned):
                staged[it, to, b] = sums[which, index_s[which * 4 + 3, to * owned + b]].astype(BF16)
            copies.append(
                pltpu.make_async_remote_copy(
                    staged.at[it, to], landed.at[it, here], send.at[it, n], recv.at[it, n],
                    device_id=place(to), device_id_type=MESH,
                )
            )
            copies[-1].start()
        return copies

    def send_gram(it, part, landed, size, here, send, recv, place):
        landed[it, here] = part
        copies = []
        for n in range(1, size):
            copies.append(
                pltpu.make_async_remote_copy(
                    landed.at[it, here], landed.at[it, here], send.at[it, n], recv.at[it, n],
                    device_id=place(lax.rem(here + n, size)), device_id_type=MESH,
                )
            )
            copies[-1].start()
        return copies

    def add_gram(it, copies, landed, size):
        for copy in copies:
            copy.wait()
        total = landed[it, 0]
        for n in range(1, size):
            total = total + landed[it, n]
        return total

    def gram_begin(it, image):
        gram = lax.dot_general(image, image, NT, precision=HIGH, preferred_element_type=F32)
        packed = jnp.concatenate([gram[n * 8 : n * 8 + 8] for n in range(k // 8)], axis=1)
        return send_gram(it, packed, gram_row, grid_rows, r, gram_row_send, gram_row_recv, lambda to: (to, c))

    def gram_middle(it, copies):
        packed = add_gram(it, copies, gram_row, grid_rows)
        return send_gram(it, packed, gram_col, grid_cols, c, gram_col_send, gram_col_recv, lambda to: (r, to))

    def gram_end(it, copies):
        packed = add_gram(it, copies, gram_col, grid_cols)
        gram = jnp.concatenate([packed[:, n * k : n * k + k] for n in range(k // 8)], axis=0)
        return inverse_factor(gram * (1.0 / total_rows))

    def normalise(inverse, image):
        return lax.dot_general(inverse, image, NN, precision=HIGH, preferred_element_type=F32)

    def turn_chunks(first, end):
        for n in range(first, end):
            block_copies[n].wait()

            def turn(m, _, n=n):
                turned[n * per_chunk + m] = held[n * per_chunk + m].T
                return 0

            lax.fori_loop(0, per_chunk, turn, 0, unroll=True)

    for it in range(ITERS):
        sent = share(it, image)
        if it == 0:
            for copy in block_copies:
                copy.start()
        if it > 0:
            gram_copies = gram_begin(it - 1, image)
        if it == 0:
            turn_chunks(0, EARLY_CHUNKS)
        pass_on(it, sent)
        if it == 0:
            turn_chunks(EARLY_CHUNKS, CHUNKS)
            index_copy.wait()
        finish(sent, "col")
        if it > 0:
            gram_copies = gram_middle(it - 1, gram_copies)
        multiply(0, turned, col_vecs, it)
        row_moves = spread(
            it, 0, grid_cols, c, row_out, row_in, row_out_send, row_out_recv, lambda to: (r, to)
        )
        finish(sent, "row")
        multiply(1, held, row_vecs, it)
        col_moves = spread(
            it, 1, grid_rows, r, col_out, col_in, col_out_send, col_out_recv, lambda to: (to, c)
        )
        parts = []
        for b in range(owned):
            part = image[:, b * side : (b + 1) * side]
            weight = weight_ref[pl.ds(b * side, side)].reshape(1, side)
            parts.append(
                part * weight + sums[0, index_s[3, c * owned + b]] + sums[1, index_s[7, r * owned + b]]
            )
        if it > 0:
            inverse = gram_end(it - 1, gram_copies)
        for n in range(1, grid_rows):
            col_moves[n - 1].wait()
            at = row_peer(grid_rows - n)
            for b in range(owned):
                parts[b] = parts[b] + col_in[it, at, b].astype(F32)
        for n in range(1, grid_cols):
            row_moves[n - 1].wait()
            at = col_peer(grid_cols - n)
            for b in range(owned):
                parts[b] = parts[b] + row_in[it, at, b].astype(F32)
        image = jnp.concatenate(parts, axis=1)
        if it > 0:
            image = normalise(inverse, image)
    last = ITERS - 1
    inverse = gram_end(last, gram_middle(last, gram_begin(last, image)))
    out_ref[...] = normalise(inverse, image)


def solution(mesh):
    grid_rows, grid_cols = mesh.shape["row"], mesh.shape["col"]

    def shards(start, self_weight, blocks, slot_row, slot_col, slot_count):
        rows, k = start.shape
        slots, side = blocks.shape[2], blocks.shape[3]
        owned = rows // side
        group_rows, group_cols = owned * grid_cols, owned * grid_rows
        total_rows = rows * grid_rows * grid_cols
        any_space = pl.BlockSpec(memory_space=pl.ANY)
        vmem = pl.BlockSpec(memory_space=pltpu.VMEM)
        dma = pltpu.SemaphoreType.DMA
        turned = pl.pallas_call(
            functools.partial(kernel, grid_rows, grid_cols, total_rows),
            out_shape=jax.ShapeDtypeStruct((k, rows), F32),
            in_specs=[any_space, vmem, any_space, vmem, vmem, pl.BlockSpec(memory_space=pltpu.SMEM)],
            out_specs=vmem,
            scratch_shapes=[
                pltpu.VMEM((k, rows), F32),
                pltpu.VMEM((slots, side, side), BF16),
                pltpu.VMEM((slots, side, side), BF16),
                pltpu.VMEM((8, slots), jnp.int32),
                pltpu.SMEM((8, slots), jnp.int32),
                [pltpu.VMEM((grid_cols, owned, k, side), BF16)] * ITERS,
                [pltpu.VMEM((grid_rows, owned, k, side), BF16)] * ITERS,
                pltpu.VMEM((2, slots + 1, k, side), F32),
                pltpu.VMEM((ITERS, grid_cols, owned, k, side), BF16),
                pltpu.VMEM((ITERS, grid_rows, owned, k, side), BF16),
                pltpu.VMEM((ITERS, grid_cols, owned, k, side), BF16),
                pltpu.VMEM((ITERS, grid_rows, owned, k, side), BF16),
                pltpu.VMEM((ITERS, grid_rows, 8, k * k // 8), F32),
                pltpu.VMEM((ITERS, grid_cols, 8, k * k // 8), F32),
                dma,
                dma((CHUNKS,)),
                dma,
            ]
            + [dma((ITERS, n)) for n in (grid_cols, grid_cols, grid_rows, grid_rows)] * 2
            + [dma((ITERS, n)) for n in (grid_rows, grid_rows, grid_cols, grid_cols)],
            compiler_params=pltpu.CompilerParams(
                collective_id=0, has_side_effects=True, vmem_limit_bytes=60 * 2**20
            ),
        )(
            start.T,
            self_weight,
            blocks.reshape(slots, side, side),
            slot_row.reshape(1, 1, slots),
            slot_col.reshape(1, 1, slots),
            slot_count,
        )
        return turned.T

    placed = (
        P(("row", "col"), None),
        P(("row", "col")),
        P("row", "col", None, None, None),
        P("row", "col", None),
        P("row", "col", None),
        P("row", "col"),
    )
    return jax.shard_map(
        shards, mesh=mesh, in_specs=placed, out_specs=P(("row", "col"), None), check_vma=False
    )
```
